128 devices in a mesh: occ: 8 (over x, core), vir: 16 (over y, z).
Axes of the slice: x: 4, y: 4, z: 4, core: 2. Of those that a mesh axis runs over, the one named last changes fastest.
Arguments:
- right_prev: bfloat16 [8192, 32768], P(None, ('vir', 'occ')), may hold values from -6 to 6
- amplitudes: bfloat16 [8192, 8192], P('occ', 'vir'), may hold values from -6 to 6
- integrals: bfloat16 [16, 4096, 2048], P('vir'), may hold values from -0.09375 to 0.09375
- send_tiles: int32 [16, 16, 2], replicated, may hold values from 0 to 3, as said below
- pair_count: int32 [16, 16], replicated, may hold values from 0 to 2, as said below
Outputs:
- residual: float32 [8192, 32768], P(None, ('vir', 'occ'))
The draws below stay inside these ranges and needn't reach their ends.
Inputs may be any that keep to these rules, and one draw needn't show every extreme that they name: `send_tiles`: the 2 slots of one sender and one owner name distinct tiles. `pair_count`: one owner receives 2 live slots from every sender.
All inputs are finite; a program needn't handle non-finite values.
Results may differ from the reference program's by a relative error of at most 0.0017.
Values may be sent and summed in bfloat16 or wider, within the bound.
No kernel may reach another device: no remote copies, remote signals or barrier semaphores. Data moves between devices by JAX's collectives and lax.ppermute only.
A program may use at most 128 MiB of HBM per device.

```python
import jax
import jax.numpy as jnp
from jax import lax

TILE = 128
VT_DEV = 4
AT_DEV = 16
CAP = 2
SLOTS = 32
NROWS = 8192
NVT = 64
NA = 32768
N_VIR = 16


def pair_helper(key):
    heavy_key, count_key, order_key = jax.random.split(key, 3)
    heavy = jax.random.randint(heavy_key, (), 0, N_VIR)
    counts = jax.random.randint(count_key, (N_VIR, N_VIR), 0, CAP + 1)
    filled = jnp.arange(N_VIR)[None, :] == heavy
    counts = jnp.where(filled, CAP, counts).astype(jnp.int32)
    scores = jax.random.randint(order_key, (N_VIR, N_VIR, VT_DEV), 0, 1 << 20) * VT_DEV + jnp.arange(VT_DEV)
    order = jnp.argsort(scores, axis=-1)[..., :CAP].astype(jnp.int32)
    return (counts, order)


def draw_pair_count(key, part):
    return pair_helper(key)[0]


def draw_send_tiles(key, part):
    return pair_helper(key)[1]


def steps_of(stream_key, extent, cuts, least, high):
    level, own = 1.0, jax.random.fold_in(stream_key, 6)
    for axis_at, parts in cuts:
        draws = jnp.exp(jax.random.uniform(jax.random.fold_in(own, axis_at), (parts,), jnp.float32, least / len(cuts), high / len(cuts)))
        level = level * jnp.repeat(draws, extent[axis_at] // parts).reshape([-1 if axis == axis_at else 1 for axis in range(len(extent))])
    return level


def centred(own_key, shape, deviation, bound, shards=(), kind=jnp.bfloat16):
    array = deviation * jax.random.normal(own_key, shape, jnp.float32)
    if shards:
        array = array * steps_of(own_key, shape, shards, -0.22, 0.18)
    return jnp.clip(array, -bound, bound).astype(kind)


def setup_inputs(seed: int = 0) -> dict:
    streams_of = jax.random.split(jax.random.key(seed), 6)
    return {
        "right_prev": centred(streams_of[0], (NROWS, NA), 1.0, 6.0, ((1, 128),)),
        "amplitudes": centred(streams_of[1], (NROWS, NVT * TILE), 1.0, 6.0, ((0, 8), (1, 16))),
        "integrals": centred(streams_of[2], (N_VIR, SLOTS * TILE, AT_DEV * TILE), (SLOTS * TILE) ** -0.5, 0.09375, ((0, 16),)),
        "send_tiles": draw_send_tiles(jax.random.fold_in(streams_of[5], 71), 0),
        "pair_count": draw_pair_count(jax.random.fold_in(streams_of[5], 71), 0),
    }


def reference(right_prev, amplitudes, integrals, send_tiles, pair_count):
    amp_tiles = amplitudes.reshape(NROWS, NVT, TILE)
    slot_ids = jnp.arange(CAP, dtype=jnp.int32)
    senders = jnp.arange(N_VIR, dtype=jnp.int32)

    def owner_term(target):
        chosen = send_tiles[:, target, :]
        counts = pair_count[:, target]
        columns = (senders[:, None] * VT_DEV + chosen).reshape(-1).astype(jnp.int32)
        live_slots = (slot_ids[None, :] < counts[:, None]).reshape(-1)
        picked = jnp.take(amp_tiles, columns, axis=1)
        picked = jnp.where(live_slots[None, :, None], picked, jnp.zeros_like(picked))
        picked = picked.reshape(NROWS, SLOTS * TILE)
        return jnp.dot(picked, integrals[target], preferred_element_type=jnp.float32).astype(jnp.bfloat16)

    ladder = lax.map(owner_term, senders)
    ladder = jnp.transpose(ladder, (1, 0, 2)).reshape(NROWS, NA)
    return right_prev.astype(jnp.float32) + ladder.astype(jnp.float32)
```

```python
import functools

import jax
import jax.numpy as jnp
from jax import lax
from jax.experimental import pallas as pl
from jax.experimental.pallas import tpu as pltpu
from jax.sharding import PartitionSpec as P

TILE = 128
CAP = 2
WAVES = ((256, 256), (256, 256))
NV = 16
NX = 4
YA, YB, ZA, ZB = 4, 12, 1, 3
ORDERS = (
    ((YA, YB, ZA, ZB), (ZA, ZB, YA, YB)),
    ((YB, YA, ZB, ZA), (ZB, ZA, YB, YA)),
)
HOPS = (2, 1, 3, 0)
VMEM = pl.BlockSpec(memory_space=pltpu.VMEM)
SMEM = pl.BlockSpec(memory_space=pltpu.SMEM)
ANY = pl.BlockSpec(memory_space=pl.ANY)


def flip(array, masks):
    pairs = [
        (o * NV + v, o * NV + (v ^ masks[o % 2]))
        for o in range(2 * NX)
        for v in range(NV)
    ]
    return lax.ppermute(array, ("occ", "vir"), pairs)


def hop(array, dx):
    pairs = [(o, (o + 2 * dx) % (2 * NX)) for o in range(2 * NX)]
    return lax.ppermute(array, "occ", pairs)


def swap(array):
    return lax.ppermute(array, "occ", [(o, o ^ 1) for o in range(2 * NX)])


def after(value, *others):
    return lax.optimization_barrier((value, *others))[0]


def near_memory(array):
    return pltpu.with_memory_space_constraint(array, pltpu.VMEM)


def sources(me, masks, core):
    d = [jnp.where(core == 0, masks[0][i], masks[1][i]) for i in range(3)]
    out = []
    for p in range(8):
        s = me
        for bit in range(3):
            if p >> bit & 1:
                s = s ^ d[bit]
        out.append(s)
    return out


def pack_kernel(masks, meta, sent, near, far, out):
    me, core = meta[0], meta[1]
    partner = me ^ jnp.where(core == 0, masks[0][3], masks[1][3])
    for p, s in enumerate(sources(me, masks, core)):
        for k in range(CAP):
            t = sent[(s * NV + partner) * CAP + k]
            ref = near if p < 4 else far
            out[p * CAP + k] = ref[(p % 4) * 4 + t]


def pack(meta, sent, near, far, masks):
    return pl.pallas_call(
        functools.partial(pack_kernel, masks),
        out_shape=pltpu.VMEM((16, near.shape[1], TILE), near.dtype),
        in_specs=[SMEM, SMEM, VMEM, VMEM],
        out_specs=VMEM,
        cost_estimate=pl.CostEstimate(
            flops=0, bytes_accessed=4 * near.size, transcendentals=0
        ),
        compiler_params=pltpu.CompilerParams(vmem_limit_bytes=8 << 20),
        name="pack",
    )(meta, sent, near_memory(near), near_memory(far))


def ladder_kernel(masks, meta, sent, live, near, far, last, weights, *refs):
    outs, lhs = refs[:4], refs[4]
    me, core = meta[0], meta[1]
    d4 = jnp.where(core == 0, masks[0][3], masks[1][3])
    for p, s in enumerate(sources(me, masks, core)):
        ref = near if p < 4 else far
        for k in range(CAP):
            t = sent[(s * NV + me) * CAP + k]
            for sender, tile in (
                (s, ref[(p % 4) * 4 + t]),
                (s ^ d4, last[p * CAP + k]),
            ):
                at = pl.multiple_of((sender * CAP + k) * TILE, TILE)
                keep = k < live[sender * NV + me]
                lhs[:, pl.ds(at, TILE)] = jnp.where(keep, tile, jnp.zeros_like(tile))
    width = weights.shape[1] // NX
    half = width // 2
    for j, dx in enumerate(HOPS):
        at = pl.multiple_of((meta[2] + dx) % NX * width, width)
        product = jnp.dot(
            lhs[...], weights[:, pl.ds(at, width)], preferred_element_type=jnp.float32
        ).astype(jnp.bfloat16)
        outs[j][core] = product[:, :half]
        outs[j][1 - core] = product[:, half:]


def ladder(meta, sent, live, near, far, last, weights, masks):
    rows, depth, width = near.shape[1], weights.shape[0], weights.shape[1] // 8
    return pl.pallas_call(
        functools.partial(ladder_kernel, masks),
        out_shape=[pltpu.VMEM((2, rows, width), jnp.bfloat16)] * 4,
        in_specs=[SMEM] * 3 + [VMEM] * 4,
        out_specs=[VMEM] * 4,
        scratch_shapes=[pltpu.VMEM((rows, depth), jnp.bfloat16)],
        cost_estimate=pl.CostEstimate(
            flops=2 * rows * depth * width * 8,
            bytes_accessed=2 * rows * depth,
            transcendentals=0,
        ),
        compiler_params=pltpu.CompilerParams(vmem_limit_bytes=12 << 20),
        name="ladder",
    )(meta, sent, live, near_memory(near), near_memory(far), near_memory(last), weights)


def add_kernel(base, n_rows, meta, prev, m0, m1, m2, m3, swapped, *refs):
    out, sums, sems = refs[-3:]
    rows = sums.shape[1]
    moved = (m0, m1, m2, m3)
    copies = []
    for j, dx in enumerate(HOPS):
        for b in range(2):
            source = (meta[2] + NX - dx) % NX * 2 + (meta[1] ^ b)
            at = pl.ds(pl.multiple_of(source * n_rows + base, 64), rows)
            block = moved[j][0] if b == 0 else swapped[j]
            i = 2 * j + b
            sums[i] = prev[at].astype(jnp.float32) + block.astype(jnp.float32)
            copy = pltpu.make_async_copy(sums.at[i], out.at[at], sems.at[i])
            copy.start()
            copies.append(copy)
    for copy in copies:
        copy.wait()


def add(meta, prev, pieces, swapped, total, base, n_rows):
    rows, width = swapped.shape[1], swapped.shape[2]
    args = [meta, prev, *map(near_memory, pieces), near_memory(swapped)]
    specs = [SMEM] + [VMEM] * 6
    aliases = {}
    if total is not None:
        aliases = {len(args): 0}
        args.append(total)
        specs.append(ANY)
    return pl.pallas_call(
        functools.partial(add_kernel, base, n_rows),
        out_shape=jax.ShapeDtypeStruct(prev.shape, jnp.float32),
        in_specs=specs,
        out_specs=ANY,
        scratch_shapes=[
            pltpu.VMEM((8, rows, width), jnp.float32),
            pltpu.SemaphoreType.DMA((8,)),
        ],
        input_output_aliases=aliases,
        cost_estimate=pl.CostEstimate(
            flops=8 * rows * width, bytes_accessed=32 * rows * width, transcendentals=0
        ),
        compiler_params=pltpu.CompilerParams(vmem_limit_bytes=8 << 20),
        name="residual",
    )(*args)


def local(right_prev, amplitudes, integrals, send_tiles, pair_count):
    n_rows = amplitudes.shape[0]
    occ, vir = lax.axis_index("occ"), lax.axis_index("vir")
    meta = jnp.stack([vir, occ % 2, occ // 2]).astype(jnp.int32)
    sent, live = send_tiles.reshape(-1), pair_count.reshape(-1)
    weights = near_memory(integrals[0])
    prev = near_memory(right_prev)
    tiles = amplitudes.reshape(n_rows, 4, TILE).transpose(1, 0, 2)

    waves = []
    base = 0
    for sizes in WAVES:
        wave = []
        for masks, rows in zip(ORDERS, sizes):
            step = [(masks[0][i], masks[1][i]) for i in range(4)]
            wave.append([masks, step, base, tiles[:, base : base + rows]])
            base += rows
        waves.append(wave)
    total = None
    earlier = [()] * 3
    for wave in waves:
        helds, fars, results = [w[3] for w in wave], [], []
        for i in range(2):
            got = [flip(after(h, *earlier[i]), w[1][i]) for w, h in zip(wave, helds)]
            earlier[i] = got
            helds = [jnp.concatenate(pair) for pair in zip(helds, got)]
        fars = [flip(after(h, *earlier[2]), w[1][2]) for w, h in zip(wave, helds)]
        earlier[2] = fars
        lasts = [
            flip(pack(meta, sent, h, f, w[0]), w[1][3]) for w, h, f in zip(wave, helds, fars)
        ]
        for (masks, _, base, _), h, f, last in zip(wave, helds, fars, lasts):
            blocks = ladder(meta, sent, live, h, f, last, weights, masks)
            moved = [hop(block, dx) for block, dx in zip(blocks, HOPS) if dx]
            moved.append(blocks[3])
            swapped = swap(jnp.stack([block[1] for block in moved]))
            total = add(meta, prev, moved, swapped, total, base, n_rows)
    return total


def solution(mesh):
    in_specs = (P(None, ("vir", "occ")), P("occ", "vir"), P("vir", None, None), P(), P())
    out_specs = P(None, ("vir", "occ"))
    return jax.shard_map(local, mesh=mesh, in_specs=in_specs, out_specs=out_specs, check_vma=False)
```

```python
import functools

import jax
import jax.numpy as jnp
from jax import lax
from jax.experimental import pallas as pl
from jax.experimental.pallas import tpu as pltpu
from jax.sharding import PartitionSpec as P

TILE = 128
CAP = 2
OWN = 4
NV = 16
NX = 4
WAVES = (256, 384, 384)
STEPS = (0, 1, 3, 2)
X1, X2, OPPOSITE, HERE = (1, 3), (3, 1), (2, 2), (0, 0)
VMEM = pl.BlockSpec(memory_space=pltpu.VMEM)
SMEM = pl.BlockSpec(memory_space=pltpu.SMEM)
ANY = pl.BlockSpec(memory_space=pl.ANY)
SHORT = pl.CostEstimate(flops=0, bytes_accessed=1024, transcendentals=0)


def moved(vir, along_y, d):
    return jnp.where(along_y, (vir + 4 * d) & 15, (vir & 12) | ((vir + d) & 3))


def send(array, phase, d):
    def target(o, v):
        y, z = divmod(v, 4)
        return (y + d) % 4 * 4 + z if o % 2 == phase else y * 4 + (z + d) % 4

    pairs = [(o * NV + v, o * NV + target(o, v)) for o in range(2 * NX) for v in range(NV)]
    return lax.ppermute(array, ("occ", "vir"), pairs)


def flip_x(array, masks):
    return lax.ppermute(array, "occ", [(o, o ^ 2 * masks[o % 2]) for o in range(2 * NX)])


def swap(array):
    return lax.ppermute(array, "occ", [(o, o ^ 1) for o in range(2 * NX)])


def far_memory(array):
    return pltpu.with_memory_space_constraint(array, pltpu.HBM)


def by_core(core, masks):
    return masks[0] if masks[0] == masks[1] else jnp.where(core == 0, masks[0], masks[1])


def call(kernel, name, args, outs, scratch=(), weights=None, gates=(), limit=10 << 20, flops=0):
    specs = [SMEM if jnp.issubdtype(a.dtype, jnp.integer) else VMEM for a in args]
    if weights is not None:
        args, specs = [*args, far_memory(weights)], [*specs, ANY]
    n = len(args)
    specs += [ANY] * len(gates)

    def body(*refs):
        kernel(*refs[:n], *refs[n + len(gates) :])

    return pl.pallas_call(
        body,
        out_shape=[jax.ShapeDtypeStruct(shape, jnp.bfloat16) for shape in outs],
        in_specs=specs,
        out_specs=[VMEM] * len(outs),
        scratch_shapes=list(scratch),
        cost_estimate=pl.CostEstimate(flops=flops, bytes_accessed=1024, transcendentals=0),
        compiler_params=pltpu.CompilerParams(vmem_limit_bytes=limit),
        name=name,
    )(*args, *gates)


def choose(pieces):
    def kernel(*refs):
        for i, ((_, k), ref) in enumerate(zip(pieces, refs)):
            refs[-1][i] = ref[k]

    outs = [(len(pieces), *pieces[0][0].shape[1:])]
    return call(kernel, "choose", [p for p, _ in pieces], outs)[0]


def pack(meta, sent, held, at, rows, gates=()):
    def kernel(meta, sent, *refs):
        me, core = meta[0], meta[1]
        for d, out in zip(STEPS[1:], refs[4:]):
            target = moved(me, core == 1, d)
            for j, (ref, step) in enumerate(zip(refs, STEPS)):
                sender = moved(me, core == 0, 4 - step)
                for k in range(CAP):
                    t = sent[(sender * NV + target) * CAP + k]
                    q = j * CAP + k
                    tile = ref[pl.ds(at, rows), pl.ds(pl.multiple_of(t * TILE, TILE), TILE)]
                    out[q // OWN, :, pl.ds(q % OWN * TILE, TILE)] = tile

    width = held[0].shape[1]
    return call(kernel, "pack", [meta, sent, *held], [(2, rows, width)] * 3, gates=gates, limit=16 << 20)


def fetch(meta, weights, held, sems, chips):
    width = held.shape[2]
    copies = []
    for j, masks in enumerate(chips):
        at = pl.multiple_of((meta[2] ^ by_core(meta[1], masks)) * width, width)
        copy = pltpu.make_async_copy(weights.at[:, pl.ds(at, width)], held.at[j], sems.at[j])
        copy.start()
        copies.append(copy)
    return copies


def dots(meta, lhs, held, copies, outs):
    half = held.shape[2] // 2
    core = meta[1]
    for j, (copy, out) in enumerate(zip(copies, outs)):
        copy.wait()
        product = jnp.dot(
            lhs[...], held[j], preferred_element_type=jnp.float32
        ).astype(jnp.bfloat16)
        out[core] = product[:, :half]
        out[1 - core] = product[:, half:]


def room(weights, chips):
    depth, width = weights.shape
    return [
        pltpu.VMEM((len(chips), depth, width // NX), jnp.bfloat16),
        pltpu.SemaphoreType.DMA((len(chips),)),
    ]


def receive(meta, sent, live, lhs, held, packed, start):
    me, core = meta[0], meta[1]
    for i, d in enumerate(STEPS):
        for j, step in enumerate(STEPS):
            sender = moved(moved(me, core == 0, 4 - step), core == 1, 4 - d)
            for k in range(CAP):
                if i == 0:
                    t = sent[(sender * NV + me) * CAP + k]
                    tile = held[j][
                        pl.ds(start, lhs.shape[0]), pl.ds(pl.multiple_of(t * TILE, TILE), TILE)
                    ]
                else:
                    q = j * CAP + k
                    tile = packed[i - 1][q // OWN, :, pl.ds(q % OWN * TILE, TILE)]
                at = pl.multiple_of((sender * CAP + k) * TILE, TILE)
                keep = k < live[sender * NV + me]
                lhs[:, pl.ds(at, TILE)] = jnp.where(keep, tile, jnp.zeros_like(tile))


def ladder_far(meta, sent, live, held, packed, start, weights, gates=()):
    chips = (OPPOSITE, X1, X2)

    def kernel(meta, sent, live, *refs):
        weights, lhs, out0, out1, out2, buffer, sems = refs[7:]
        copies = fetch(meta, weights, buffer, sems, chips)
        receive(meta, sent, live, lhs, refs[:4], refs[4:7], start)
        dots(meta, lhs, buffer, copies, (out0, out1, out2))

    rows, (depth, width) = packed[0].shape[1], weights.shape
    outs = [(rows, depth)] + [(2, rows, width // (2 * NX))] * 3
    args = [meta, sent, live, *held, *packed]
    return call(kernel, "ladder_far", args, outs, room(weights, chips), weights, gates, 34 << 20)


def ladder_here(meta, lhs, weights, gates=()):
    def kernel(meta, lhs, weights, out, buffer, sems):
        dots(meta, lhs, buffer, fetch(meta, weights, buffer, sems, (HERE,)), (out,))

    (rows, depth), width = lhs.shape, weights.shape[1]
    outs = [(2, rows, width // (2 * NX))]
    flops = rows * depth * width // 2
    return call(
        kernel, "ladder_here", [meta, lhs], outs, room(weights, (HERE,)), weights, gates, 16 << 20, flops
    )[0]


def add(meta, prev, pieces, swapped, total, base, n_rows):
    def kernel(meta, prev, p0, p1, p2, p3, swapped, *refs):
        out, sums, sems = refs[-3:]
        core, rows = meta[1], sums.shape[1]
        copies = []
        for j, (masks, ref) in enumerate(zip((HERE, X1, X2, OPPOSITE), (p0, p1, p2, p3))):
            for b in range(2):
                chip = meta[2] ^ by_core(core ^ b, masks)
                at = pl.ds(pl.multiple_of((chip * 2 + (core ^ b)) * n_rows + base, 32), rows)
                block = swapped[j] if b else ref[pieces[j][1]]
                n = j * 2 + b
                sums[n] = prev[at].astype(jnp.float32) + block.astype(jnp.float32)
                copy = pltpu.make_async_copy(sums.at[n], out.at[at], sems.at[n])
                copy.start()
                copies.append(copy)
        for copy in copies:
            copy.wait()

    rows, width = swapped.shape[1:]
    args = [meta, prev, *(p for p, _ in pieces), swapped]
    specs = [SMEM] + [VMEM] * 6
    aliases = {}
    if total is not None:
        aliases = {len(args): 0}
        args.append(total)
        specs.append(ANY)
    return pl.pallas_call(
        kernel,
        out_shape=jax.ShapeDtypeStruct(prev.shape, jnp.float32),
        in_specs=specs,
        out_specs=ANY,
        scratch_shapes=[
            pltpu.VMEM((8, rows, width), jnp.float32),
            pltpu.SemaphoreType.DMA((8,)),
        ],
        input_output_aliases=aliases,
        cost_estimate=SHORT,
        compiler_params=pltpu.CompilerParams(vmem_limit_bytes=18 << 20),
        name="residual",
    )(*args)


def local(right_prev, amplitudes, integrals, send_tiles, pair_count):
    n_rows = amplitudes.shape[0]
    occ, vir = lax.axis_index("occ"), lax.axis_index("vir")
    meta = jnp.stack([vir, occ % 2, occ // 2]).astype(jnp.int32)
    sent, live = send_tiles.reshape(-1), pair_count.reshape(-1)
    weights = integrals[0]

    held = [amplitudes] + [send(amplitudes, 0, d) for d in STEPS[1:]]
    starts = [sum(WAVES[:i]) for i in range(len(WAVES))]
    waves, gates = [], ()
    for start, rows in zip(starts, WAVES):
        packed = pack(meta, sent, held, start, rows, gates)
        waves.append([send(v, 1, d) for v, d in zip(packed, STEPS[1:])])
        gates = packed[:1]

    moved_blocks, results = (), []
    for got, start in zip(waves, starts):
        lhs, *sends = ladder_far(meta, sent, live, held, got, start, weights, gates)
        blocks = [flip_x(v, m) for v, m in zip(sends, (OPPOSITE, X1, X2))]
        here = ladder_here(meta, lhs, weights, moved_blocks)
        moved_blocks, gates = blocks, (here,)
        results.append([(here, 0), (blocks[1], 0), (blocks[2], 0), (blocks[0], 0)])

    total = None
    for pieces, start in zip(results, starts):
        swapped = swap(choose([(p, i + 1) for p, i in pieces]))
        total = add(meta, right_prev, pieces, swapped, total, start, n_rows)
    return total


def solution(mesh):
    in_specs = (P(None, ("vir", "occ")), P("occ", "vir"), P("vir", None, None), P(), P())
    out_specs = P(None, ("vir", "occ"))
    return jax.shard_map(local, mesh=mesh, in_specs=in_specs, out_specs=out_specs, check_vma=False)
```

```python
import functools

import jax
import jax.numpy as jnp
from jax import lax
from jax.experimental import pallas as pl
from jax.experimental.pallas import tpu as pltpu
from jax.sharding import PartitionSpec as P

TILE = 128
CAP = 2
OWN = 4
NV = 16
NX = 4
GROUPS = ((256,), (384, 384))
STEPS = (0, 1, 3, 2)
X1, X2, OPPOSITE, HERE = (1, 3), (3, 1), (2, 2), (0, 0)
VMEM = pl.BlockSpec(memory_space=pltpu.VMEM)
SMEM = pl.BlockSpec(memory_space=pltpu.SMEM)
ANY = pl.BlockSpec(memory_space=pl.ANY)
SHORT = pl.CostEstimate(flops=0, bytes_accessed=1024, transcendentals=0)


def moved(vir, along_y, d):
    return jnp.where(along_y, (vir + 4 * d) & 15, (vir & 12) | ((vir + d) & 3))


def send(array, phase, d):
    def target(o, v):
        y, z = divmod(v, 4)
        return (y + d) % 4 * 4 + z if o % 2 == phase else y * 4 + (z + d) % 4

    pairs = [(o * NV + v, o * NV + target(o, v)) for o in range(2 * NX) for v in range(NV)]
    return lax.ppermute(array, ("occ", "vir"), pairs)


def flip_x(array, masks):
    return lax.ppermute(array, "occ", [(o, o ^ 2 * masks[o % 2]) for o in range(2 * NX)])


def swap(array):
    return lax.ppermute(array, "occ", [(o, o ^ 1) for o in range(2 * NX)])


def far_memory(array):
    return pltpu.with_memory_space_constraint(array, pltpu.HBM)


def by_core(core, masks):
    return masks[0] if masks[0] == masks[1] else jnp.where(core == 0, masks[0], masks[1])


def call(kernel, name, args, outs, scratch=(), weights=None, gates=(), limit=10 << 20, flops=0):
    specs = [SMEM if jnp.issubdtype(a.dtype, jnp.integer) else VMEM for a in args]
    if weights is not None:
        args, specs = [*args, far_memory(weights)], [*specs, ANY]
    n = len(args)
    specs += [ANY] * len(gates)

    def body(*refs):
        kernel(*refs[:n], *refs[n + len(gates) :])

    return pl.pallas_call(
        body,
        out_shape=[jax.ShapeDtypeStruct(shape, jnp.bfloat16) for shape in outs],
        in_specs=specs,
        out_specs=[VMEM] * len(outs),
        scratch_shapes=list(scratch),
        cost_estimate=pl.CostEstimate(flops=flops, bytes_accessed=1024, transcendentals=0),
        compiler_params=pltpu.CompilerParams(vmem_limit_bytes=limit),
        name=name,
    )(*args, *gates)


def cut(amplitudes, at, rows, gates=()):
    def kernel(source, *refs):
        out, sem = refs[-2:]
        copy = pltpu.make_async_copy(source.at[pl.ds(at, rows)], out, sem)
        copy.start()
        copy.wait()

    return pl.pallas_call(
        kernel,
        out_shape=jax.ShapeDtypeStruct((rows, amplitudes.shape[1]), amplitudes.dtype),
        in_specs=[ANY] * (1 + len(gates)),
        out_specs=VMEM,
        scratch_shapes=[pltpu.SemaphoreType.DMA],
        cost_estimate=SHORT,
        compiler_params=pltpu.CompilerParams(vmem_limit_bytes=4 << 20),
        name="cut",
    )(far_memory(amplitudes), *gates)


def choose(pieces):
    def kernel(*refs):
        for i, ((_, k), ref) in enumerate(zip(pieces, refs)):
            refs[-1][i] = ref[k]

    outs = [(len(pieces), *pieces[0][0].shape[1:])]
    return call(kernel, "choose", [p for p, _ in pieces], outs)[0]


def pack(meta, sent, held, at, rows, gates=()):
    def kernel(meta, sent, *refs):
        me, core = meta[0], meta[1]
        for d, out in zip(STEPS[1:], refs[4:]):
            target = moved(me, core == 1, d)
            for j, (ref, step) in enumerate(zip(refs, STEPS)):
                sender = moved(me, core == 0, 4 - step)
                for k in range(CAP):
                    t = sent[(sender * NV + target) * CAP + k]
                    q = j * CAP + k
                    tile = ref[pl.ds(at, rows), pl.ds(pl.multiple_of(t * TILE, TILE), TILE)]
                    out[q // OWN, :, pl.ds(q % OWN * TILE, TILE)] = tile

    width = held[0].shape[1]
    return call(kernel, "pack", [meta, sent, *held], [(2, rows, width)] * 3, gates=gates, limit=16 << 20)


def fetch(meta, weights, held, sems, chips):
    width = held.shape[2]
    copies = []
    for j, masks in enumerate(chips):
        at = pl.multiple_of((meta[2] ^ by_core(meta[1], masks)) * width, width)
        copy = pltpu.make_async_copy(weights.at[:, pl.ds(at, width)], held.at[j], sems.at[j])
        copy.start()
        copies.append(copy)
    return copies


def dots(meta, lhs, held, copies, outs):
    half = held.shape[2] // 2
    core = meta[1]
    for j, (copy, out) in enumerate(zip(copies, outs)):
        copy.wait()
        product = jnp.dot(
            lhs[...], held[j], preferred_element_type=jnp.float32
        ).astype(jnp.bfloat16)
        out[core] = product[:, :half]
        out[1 - core] = product[:, half:]


def room(weights, chips):
    depth, width = weights.shape
    return [
        pltpu.VMEM((len(chips), depth, width // NX), jnp.bfloat16),
        pltpu.SemaphoreType.DMA((len(chips),)),
    ]


def receive(meta, sent, live, lhs, held, packed, start):
    me, core = meta[0], meta[1]
    for i, d in enumerate(STEPS):
        for j, step in enumerate(STEPS):
            sender = moved(moved(me, core == 0, 4 - step), core == 1, 4 - d)
            for k in range(CAP):
                if i == 0:
                    t = sent[(sender * NV + me) * CAP + k]
                    tile = held[j][
                        pl.ds(start, lhs.shape[0]), pl.ds(pl.multiple_of(t * TILE, TILE), TILE)
                    ]
                else:
                    q = j * CAP + k
                    tile = packed[i - 1][q // OWN, :, pl.ds(q % OWN * TILE, TILE)]
                at = pl.multiple_of((sender * CAP + k) * TILE, TILE)
                keep = k < live[sender * NV + me]
                lhs[:, pl.ds(at, TILE)] = jnp.where(keep, tile, jnp.zeros_like(tile))


def ladder_far(meta, sent, live, held, packed, start, weights, gates=()):
    chips = (OPPOSITE, X1, X2)

    def kernel(meta, sent, live, *refs):
        weights, lhs, out0, out1, out2, buffer, sems = refs[7:]
        copies = fetch(meta, weights, buffer, sems, chips)
        receive(meta, sent, live, lhs, refs[:4], refs[4:7], start)
        dots(meta, lhs, buffer, copies, (out0, out1, out2))

    rows, (depth, width) = packed[0].shape[1], weights.shape
    outs = [(rows, depth)] + [(2, rows, width // (2 * NX))] * 3
    args = [meta, sent, live, *held, *packed]
    return call(kernel, "ladder_far", args, outs, room(weights, chips), weights, gates, 34 << 20)


def ladder_here(meta, lhs, weights, gates=()):
    def kernel(meta, lhs, weights, out, buffer, sems):
        dots(meta, lhs, buffer, fetch(meta, weights, buffer, sems, (HERE,)), (out,))

    (rows, depth), width = lhs.shape, weights.shape[1]
    outs = [(2, rows, width // (2 * NX))]
    flops = rows * depth * width // 2
    return call(
        kernel, "ladder_here", [meta, lhs], outs, room(weights, (HERE,)), weights, gates, 16 << 20, flops
    )[0]


def add(meta, prev, pieces, swapped, total, base, n_rows):
    def kernel(meta, prev, p0, p1, p2, p3, swapped, *refs):
        out, sums, sems = refs[-3:]
        core, rows = meta[1], sums.shape[1]
        copies = []
        for j, (masks, ref) in enumerate(zip((HERE, X1, X2, OPPOSITE), (p0, p1, p2, p3))):
            for b in range(2):
                chip = meta[2] ^ by_core(core ^ b, masks)
                at = pl.ds(pl.multiple_of((chip * 2 + (core ^ b)) * n_rows + base, 32), rows)
                block = swapped[j] if b else ref[pieces[j][1]]
                n = j * 2 + b
                sums[n] = prev[at].astype(jnp.float32) + block.astype(jnp.float32)
                copy = pltpu.make_async_copy(sums.at[n], out.at[at], sems.at[n])
                copy.start()
                copies.append(copy)
        for copy in copies:
            copy.wait()

    rows, width = swapped.shape[1:]
    args = [meta, prev, *(p for p, _ in pieces), swapped]
    specs = [SMEM] + [VMEM] * 6
    aliases = {}
    if total is not None:
        aliases = {len(args): 0}
        args.append(total)
        specs.append(ANY)
    return pl.pallas_call(
        kernel,
        out_shape=jax.ShapeDtypeStruct(prev.shape, jnp.float32),
        in_specs=specs,
        out_specs=ANY,
        scratch_shapes=[
            pltpu.VMEM((8, rows, width), jnp.float32),
            pltpu.SemaphoreType.DMA((8,)),
        ],
        input_output_aliases=aliases,
        cost_estimate=SHORT,
        compiler_params=pltpu.CompilerParams(vmem_limit_bytes=18 << 20),
        name="residual",
    )(*args)


def local(right_prev, amplitudes, integrals, send_tiles, pair_count):
    n_rows = amplitudes.shape[0]
    occ, vir = lax.axis_index("occ"), lax.axis_index("vir")
    meta = jnp.stack([vir, occ % 2, occ // 2]).astype(jnp.int32)
    sent, live = send_tiles.reshape(-1), pair_count.reshape(-1)
    weights = integrals[0]

    waves, hops, gates, cut_gate, base = [], (), (), (), 0
    for group in GROUPS:
        own = cut(amplitudes, base, sum(group), cut_gate)
        held = [own] + [send(own, 0, d) for d in STEPS[1:]]
        start, received = 0, []
        for rows in group:
            packed = pack(meta, sent, held, start, rows, gates)
            received.append([send(v, 1, d) for v, d in zip(packed, STEPS[1:])])
            start, gates = start + rows, packed[:1]
        start, cut_gate = 0, received[0]
        for rows, got in zip(group, received):
            lhs, *sends = ladder_far(meta, sent, live, held, got, start, weights, gates)
            blocks = [flip_x(v, m) for v, m in zip(sends, (OPPOSITE, X1, X2))]
            here = ladder_here(meta, lhs, weights, hops)
            hops, gates = blocks, (here,)
            waves.append(([(p, 0) for p in (here, blocks[1], blocks[2], blocks[0])], base + start))
            start += rows
        base += start

    total = None
    for pieces, start in waves:
        swapped = swap(choose([(p, i + 1) for p, i in pieces]))
        total = add(meta, right_prev, pieces, swapped, total, start, n_rows)
    return total


def solution(mesh):
    in_specs = (P(None, ("vir", "occ")), P("occ", "vir"), P("vir", None, None), P(), P())
    out_specs = P(None, ("vir", "occ"))
    return jax.shard_map(local, mesh=mesh, in_specs=in_specs, out_specs=out_specs, check_vma=False)
```

```python
import functools

import jax
import jax.numpy as jnp
from jax import lax
from jax.experimental import pallas as pl
from jax.experimental.pallas import tpu as pltpu
from jax.sharding import PartitionSpec as P

TILE = 128
CAP = 2
OWN = 4
NV = 16
NX = 4
GROUPS = ((256,), (384, 384))
STEPS = (0, 1, 3, 2)
X1, X2, OPPOSITE, HERE = (1, 3), (3, 1), (2, 2), (0, 0)
VMEM = pl.BlockSpec(memory_space=pltpu.VMEM)
SMEM = pl.BlockSpec(memory_space=pltpu.SMEM)
ANY = pl.BlockSpec(memory_space=pl.ANY)
SHORT = pl.CostEstimate(flops=0, bytes_accessed=1024, transcendentals=0)


def moved(vir, along_y, d):
    return jnp.where(along_y, (vir + 4 * d) & 15, (vir & 12) | ((vir + d) & 3))


def send(array, phase, d):
    def target(o, v):
        y, z = divmod(v, 4)
        return (y + d) % 4 * 4 + z if o % 2 == phase else y * 4 + (z + d) % 4

    pairs = [(o * NV + v, o * NV + target(o, v)) for o in range(2 * NX) for v in range(NV)]
    return lax.ppermute(array, ("occ", "vir"), pairs)


def flip_x(array, masks):
    return lax.ppermute(array, "occ", [(o, o ^ 2 * masks[o % 2]) for o in range(2 * NX)])


def swap(array):
    return lax.ppermute(array, "occ", [(o, o ^ 1) for o in range(2 * NX)])


def far_memory(array):
    return pltpu.with_memory_space_constraint(array, pltpu.HBM)


def by_core(core, masks):
    return masks[0] if masks[0] == masks[1] else jnp.where(core == 0, masks[0], masks[1])


def call(kernel, name, args, outs, scratch=(), weights=None, gates=(), limit=10 << 20, flops=0):
    specs = [SMEM if jnp.issubdtype(a.dtype, jnp.integer) else VMEM for a in args]
    if weights is not None:
        args, specs = [*args, far_memory(weights)], [*specs, ANY]
    n = len(args)
    specs += [ANY] * len(gates)

    def body(*refs):
        kernel(*refs[:n], *refs[n + len(gates) :])

    return pl.pallas_call(
        body,
        out_shape=[jax.ShapeDtypeStruct(shape, jnp.bfloat16) for shape in outs],
        in_specs=specs,
        out_specs=[VMEM] * len(outs),
        scratch_shapes=list(scratch),
        cost_estimate=pl.CostEstimate(flops=flops, bytes_accessed=1024, transcendentals=0),
        compiler_params=pltpu.CompilerParams(vmem_limit_bytes=limit),
        name=name,
    )(*args, *gates)


def cut(amplitudes, at, rows, gates=()):
    def kernel(source, *refs):
        out, sem = refs[-2:]
        copy = pltpu.make_async_copy(source.at[pl.ds(at, rows)], out, sem)
        copy.start()
        copy.wait()

    return pl.pallas_call(
        kernel,
        out_shape=jax.ShapeDtypeStruct((rows, amplitudes.shape[1]), amplitudes.dtype),
        in_specs=[ANY] * (1 + len(gates)),
        out_specs=VMEM,
        scratch_shapes=[pltpu.SemaphoreType.DMA],
        cost_estimate=SHORT,
        compiler_params=pltpu.CompilerParams(vmem_limit_bytes=4 << 20),
        name="cut",
    )(far_memory(amplitudes), *gates)


def choose(pieces):
    def kernel(*refs):
        for i, ((_, k), ref) in enumerate(zip(pieces, refs)):
            refs[-1][i] = ref[k]

    outs = [(len(pieces), *pieces[0][0].shape[1:])]
    return call(kernel, "choose", [p for p, _ in pieces], outs)[0]


def pack(meta, sent, held, at, rows, gates=()):
    def kernel(meta, sent, *refs):
        me, core = meta[0], meta[1]
        for d, out in zip(STEPS[1:], refs[4:]):
            target = moved(me, core == 1, d)
            for j, (ref, step) in enumerate(zip(refs, STEPS)):
                sender = moved(me, core == 0, 4 - step)
                for k in range(CAP):
                    t = sent[(sender * NV + target) * CAP + k]
                    q = j * CAP + k
                    tile = ref[pl.ds(at, rows), pl.ds(pl.multiple_of(t * TILE, TILE), TILE)]
                    out[q // OWN, :, pl.ds(q % OWN * TILE, TILE)] = tile

    width = held[0].shape[1]
    return call(kernel, "pack", [meta, sent, *held], [(2, rows, width)] * 3, gates=gates, limit=16 << 20)


def fetch(meta, weights, held, sems, chips):
    width = held.shape[2]
    copies = []
    for j, masks in enumerate(chips):
        at = pl.multiple_of((meta[2] ^ by_core(meta[1], masks)) * width, width)
        copy = pltpu.make_async_copy(weights.at[:, pl.ds(at, width)], held.at[j], sems.at[j])
        copy.start()
        copies.append(copy)
    return copies


def dots(meta, lhs, held, copies, outs):
    half = held.shape[2] // 2
    core = meta[1]
    for j, (copy, out) in enumerate(zip(copies, outs)):
        copy.wait()
        product = jnp.dot(
            lhs[...], held[j], preferred_element_type=jnp.float32
        ).astype(jnp.bfloat16)
        out[core] = product[:, :half]
        out[1 - core] = product[:, half:]


def room(weights, chips):
    depth, width = weights.shape
    return [
        pltpu.VMEM((len(chips), depth, width // NX), jnp.bfloat16),
        pltpu.SemaphoreType.DMA((len(chips),)),
    ]


def receive(meta, sent, live, lhs, held, packed, start):
    me, core = meta[0], meta[1]
    for i, d in enumerate(STEPS):
        for j, step in enumerate(STEPS):
            sender = moved(moved(me, core == 0, 4 - step), core == 1, 4 - d)
            for k in range(CAP):
                if i == 0:
                    t = sent[(sender * NV + me) * CAP + k]
                    tile = held[j][
                        pl.ds(start, lhs.shape[0]), pl.ds(pl.multiple_of(t * TILE, TILE), TILE)
                    ]
                else:
                    q = j * CAP + k
                    tile = packed[i - 1][q // OWN, :, pl.ds(q % OWN * TILE, TILE)]
                at = pl.multiple_of((sender * CAP + k) * TILE, TILE)
                keep = k < live[sender * NV + me]
                lhs[:, pl.ds(at, TILE)] = jnp.where(keep, tile, jnp.zeros_like(tile))


def ladder_far(meta, sent, live, held, packed, start, weights, gates=()):
    chips = (OPPOSITE, X1, X2)

    def kernel(meta, sent, live, *refs):
        weights, lhs, out0, out1, out2, buffer, sems = refs[7:]
        copies = fetch(meta, weights, buffer, sems, chips)
        receive(meta, sent, live, lhs, refs[:4], refs[4:7], start)
        dots(meta, lhs, buffer, copies, (out0, out1, out2))

    rows, (depth, width) = packed[0].shape[1], weights.shape
    outs = [(rows, depth)] + [(2, rows, width // (2 * NX))] * 3
    args = [meta, sent, live, *held, *packed]
    return call(kernel, "ladder_far", args, outs, room(weights, chips), weights, gates, 34 << 20)


def ladder_here(meta, lhs, weights, gates=()):
    def kernel(meta, lhs, weights, out, buffer, sems):
        dots(meta, lhs, buffer, fetch(meta, weights, buffer, sems, (HERE,)), (out,))

    (rows, depth), width = lhs.shape, weights.shape[1]
    outs = [(2, rows, width // (2 * NX))]
    flops = rows * depth * width // 2
    return call(
        kernel, "ladder_here", [meta, lhs], outs, room(weights, (HERE,)), weights, gates, 16 << 20, flops
    )[0]


def add(meta, prev, pieces, swapped, total, base, n_rows):
    def kernel(meta, prev, p0, p1, p2, p3, swapped, *refs):
        out, sums, sems = refs[-3:]
        core, rows = meta[1], sums.shape[1]
        copies = []
        for j, (masks, ref) in enumerate(zip((HERE, X1, X2, OPPOSITE), (p0, p1, p2, p3))):
            for b in range(2):
                chip = meta[2] ^ by_core(core ^ b, masks)
                at = pl.ds(pl.multiple_of((chip * 2 + (core ^ b)) * n_rows + base, 32), rows)
                block = swapped[j] if b else ref[pieces[j][1]]
                n = j * 2 + b
                sums[n] = prev[at].astype(jnp.float32) + block.astype(jnp.float32)
                copy = pltpu.make_async_copy(sums.at[n], out.at[at], sems.at[n])
                copy.start()
                copies.append(copy)
        for copy in copies:
            copy.wait()

    rows, width = swapped.shape[1:]
    args = [meta, prev, *(p for p, _ in pieces), swapped]
    specs = [SMEM] + [VMEM] * 6
    aliases = {}
    if total is not None:
        aliases = {len(args): 0}
        args.append(total)
        specs.append(ANY)
    return pl.pallas_call(
        kernel,
        out_shape=jax.ShapeDtypeStruct(prev.shape, jnp.float32),
        in_specs=specs,
        out_specs=ANY,
        scratch_shapes=[
            pltpu.VMEM((8, rows, width), jnp.float32),
            pltpu.SemaphoreType.DMA((8,)),
        ],
        input_output_aliases=aliases,
        cost_estimate=SHORT,
        compiler_params=pltpu.CompilerParams(vmem_limit_bytes=18 << 20),
        name="residual",
    )(*args)


def local(right_prev, amplitudes, integrals, send_tiles, pair_count):
    n_rows = amplitudes.shape[0]
    occ, vir = lax.axis_index("occ"), lax.axis_index("vir")
    meta = jnp.stack([vir, occ % 2, occ // 2]).astype(jnp.int32)
    sent, live = send_tiles.reshape(-1), pair_count.reshape(-1)
    weights = integrals[0]

    waves, hops, gates, cut_gate, base = [], (), (), (), 0
    for group in GROUPS:
        own = cut(amplitudes, base, sum(group), cut_gate)
        held = [own] + [send(own, 0, d) for d in STEPS[1:]]
        start, received = 0, []
        for rows in group:
            packed = pack(meta, sent, held, start, rows, gates)
            received.append([send(v, 1, d) for v, d in zip(packed, STEPS[1:])])
            start, gates = start + rows, packed[:1]
        start, cut_gate = 0, received[0]
        for rows, got in zip(group, received):
            lhs, *sends = ladder_far(meta, sent, live, held, got, start, weights, gates)
            blocks = [flip_x(v, m) for v, m in zip(sends, (OPPOSITE, X1, X2))]
            here = ladder_here(meta, lhs, weights, hops)
            hops, gates = blocks, (here,)
            waves.append(([(p, 0) for p in (here, blocks[1], blocks[2], blocks[0])], base + start))
            start += rows
        base += start

    total = None
    for pieces, start in (waves[1], waves[0], *waves[2:]):
        swapped = swap(choose([(p, i + 1) for p, i in pieces]))
        total = add(meta, right_prev, pieces, swapped, total, start, n_rows)
    return total


def solution(mesh):
    in_specs = (P(None, ("vir", "occ")), P("occ", "vir"), P("vir", None, None), P(), P())
    out_specs = P(None, ("vir", "occ"))
    return jax.shard_map(local, mesh=mesh, in_specs=in_specs, out_specs=out_specs, check_vma=False)
```
